128 devices in a mesh: grp: 64 (over z, x, y), mem: 2 (over core).
Axes of the slice: x: 4, y: 4, z: 4, core: 2. Of those that a mesh axis runs over, the one named last changes fastest.
Arguments:
- embeddings: float32 [131072, 1024], P(('grp', 'mem')), may hold values from -6 to 6
- cluster_of: int32 [131072], P(('grp', 'mem')), may hold values from 0 to 383, as said below
Outputs:
- best_similarity: float32 [131072], P(('grp', 'mem'))
The draws below stay inside these ranges and needn't reach their ends.
Inputs may be any that keep to these rules, and one draw needn't show every extreme that they name: `cluster_of`: cluster c is owned by the device of index (c mod 64) * 2 + (c // 64) mod 2, counted over grp then mem. Among the rows of one device, at most 16 lie in the clusters of one owning device; in every draw the 2 owning devices of one group receive exactly 16 rows from every device. Some clusters have a single row.
All inputs are finite; a program needn't handle non-finite values.
Results may differ from the reference program's by a relative error of at most 0.0014.
Values may be sent and summed in bfloat16 or wider, within the bound.
A program may use at most 64 MiB of HBM per device.

```python
import math
import jax
import jax.numpy as jnp
from jax import lax

D = 1024
ROWS_DEV = 1024
CL_DEV = 3
SLOT = 16
ROWS = 131072
N_GRP = 64
N_MEM = 2


def draw_cluster_of(key, part):
    key = jax.random.fold_in(key, 11)
    key_busy, key_single, key_host, key_devices = jax.random.split(key, 4)
    owner_count = N_GRP * N_MEM
    busy_group = jax.random.randint(key_busy, (), 0, N_GRP).astype(jnp.int32)
    single_layer = jax.random.randint(key_single, (N_MEM,), 0, CL_DEV).astype(jnp.int32)
    host_device = jax.random.randint(key_host, (N_MEM,), 0, owner_count).astype(jnp.int32)
    device_keys = jax.random.split(key_devices, owner_count)
    position = jnp.arange(ROWS_DEV, dtype=jnp.int32)
    busy_members = jnp.repeat(jnp.arange(N_MEM, dtype=jnp.int32), SLOT)

    def one_device(device_key, device_index):
        key_spots, key_layer, key_busy_layer, key_shuffle = jax.random.split(device_key, 4)
        spots = jax.random.permutation(key_spots, (owner_count - N_MEM) * SLOT)[:ROWS_DEV - N_MEM * SLOT]
        other_owner = ((busy_group * N_MEM + N_MEM + spots // SLOT) % owner_count).astype(jnp.int32)
        owner_index = jnp.concatenate([busy_group * N_MEM + busy_members, other_owner])
        member = owner_index % N_MEM
        group_index = owner_index // N_MEM
        free_layer = jax.random.randint(key_layer, (ROWS_DEV,), 0, CL_DEV).astype(jnp.int32)
        reduced = jax.random.randint(key_busy_layer, (ROWS_DEV,), 0, CL_DEV - 1).astype(jnp.int32)
        skipped = single_layer[member]
        busy_layer = reduced + (reduced >= skipped).astype(jnp.int32)
        layer = jnp.where(group_index == busy_group, busy_layer, free_layer)
        host_member = jnp.minimum(position // SLOT, N_MEM - 1)
        lonely = (position < N_MEM * SLOT) & (position % SLOT == 0) & (host_device[host_member] == device_index)
        layer = jnp.where(lonely, skipped, layer)
        clusters = group_index + N_GRP * (member + N_MEM * layer)
        return clusters[jax.random.permutation(key_shuffle, ROWS_DEV)].astype(jnp.int32)
    return jax.vmap(one_device)(device_keys, jnp.arange(owner_count, dtype=jnp.int32)).reshape(-1)


def levels(key, shape, cuts, least, top_value):
    factor_of, own = 1.0, jax.random.fold_in(key, 6)
    for dim, shards_of in cuts:
        steps = jnp.exp(jax.random.uniform(jax.random.fold_in(own, dim), (shards_of,), jnp.float32, least / len(cuts), top_value / len(cuts)))
        factor_of = factor_of * jnp.repeat(steps, shape[dim] // shards_of).reshape([-1 if axis == dim else 1 for axis in range(len(shape))])
    return factor_of


def normal_values(stream_key, shape, scale, reach, pieces=(), kind=jnp.bfloat16):
    factor_of = levels(stream_key, shape, pieces, -0.22, 0.18) if pieces else 1.0
    drawn = jax.random.normal(stream_key, shape, jnp.float32) * scale * factor_of
    return jnp.minimum(jnp.maximum(drawn, -reach), reach).astype(kind)


def setup_inputs(seed: int = 0) -> dict:
    arg_keys = jax.random.split(jax.random.key(seed), 3)
    return {
        "embeddings": normal_values(arg_keys[0], (ROWS, D), 1.0, 6.0, ((0, 128),), jnp.float32),
        "cluster_of": draw_cluster_of(jax.random.fold_in(arg_keys[2], 71), 0),
    }


def reference(embeddings, cluster_of):
    factor = lax.rsqrt(lax.optimization_barrier(jnp.mean(embeddings * embeddings, axis=1, keepdims=True)) + 1e-06) / math.sqrt(D)
    normed = (embeddings * factor).astype(jnp.bfloat16)
    owner_count = N_GRP * N_MEM
    owner_index = (cluster_of % N_GRP * N_MEM + cluster_of // N_GRP % N_MEM).astype(jnp.int32)
    ordering = jnp.argsort(owner_index, stable=True).astype(jnp.int32)
    counts = jnp.bincount(owner_index, length=owner_count).astype(jnp.int32)
    starts = (jnp.cumsum(counts) - counts).astype(jnp.int32)
    capacity = 2 * ROWS_DEV

    def per_owner(owner_pick):
        slot_range = jnp.arange(capacity, dtype=jnp.int32)
        position = jnp.minimum(starts[owner_pick] + slot_range, ROWS - 1).astype(jnp.int32)
        filled = slot_range < counts[owner_pick]
        members = jnp.where(filled, ordering[position], -1).astype(jnp.int32)
        safe_members = jnp.maximum(members, 0).astype(jnp.int32)
        member_rows = normed[safe_members]
        member_ids = jnp.where(filled, cluster_of[safe_members], -1).astype(jnp.int32)
        scores = jnp.dot(member_rows, member_rows.T, preferred_element_type=jnp.float32)
        allowed = (member_ids[:, None] == member_ids[None, :]) & (member_ids[:, None] >= 0) & (members[:, None] != members[None, :])
        return (lax.optimization_barrier(jnp.max(jnp.where(allowed, scores, -1.0), axis=1)), members)
    owner_best, owner_members = lax.map(per_owner, jnp.arange(owner_count, dtype=jnp.int32))
    targets = jnp.where(owner_members >= 0, owner_members, ROWS).reshape(-1).astype(jnp.int32)
    result = jnp.full((ROWS,), -1.0, jnp.float32).at[targets].set(owner_best.reshape(-1), mode='drop')
    return result
```

```python
import functools
import math

import jax
import jax.numpy as jnp
from jax import lax
from jax.experimental import pallas as pl
from jax.experimental.pallas import tpu as pltpu
from jax.sharding import PartitionSpec as P

MESH = pl.DeviceIdType.MESH
STEP = 115
BACK = 59
DEVS = 128
SLOT = 16
GROUP = 16
CHUNK = GROUP * SLOT
CHUNKS = DEVS // GROUP
NT = (((1,), (1,)), ((), ()))


def dot(a, b, dims=(((1,), (0,)), ((), ()))):
    return lax.dot_general(a, b, dims, preferred_element_type=jnp.float32)


def iota(shape, dim):
    return lax.broadcasted_iota(jnp.int32, shape, dim)


def kernel(
    emb, ids, out,
    raw, normed, send, recv, tag_out, tag_in, best_out, best_in,
    tag_col, tag_row, row_max, col_max,
    load_sem, send_sem, recv_sem, tag_sems, best_sems,
):
    rows, width = raw.shape
    grp, core = lax.axis_index("grp"), lax.axis_index("mem")
    z, x, y = grp // 16, (grp // 4) % 4, grp % 4

    def shift(k):
        q = (k * STEP) % DEVS
        return q // 32, (q // 8) % 4, (q // 2) % 4, q % 2

    def to(k):
        dz, dx, dy, dc = shift(k)
        way = 1 - 2 * core
        g = ((z + way * dz + 4) % 4) * 16 + ((x + way * dx + 4) % 4) * 4 + (y + way * dy + 4) % 4
        return g, (core + dc) % 2

    def origin(k):
        dz, dx, dy, dc = shift(k)
        there = (core + dc) % 2
        way = 1 - 2 * there
        g = ((z - way * dz + 4) % 4) * 16 + ((x - way * dx + 4) % 4) * 4 + (y - way * dy + 4) % 4
        return g, there

    part = rows // 8
    loads = [
        pltpu.make_async_copy(
            emb.at[pl.ds(i * part, part)], raw.at[pl.ds(i * part, part)], load_sem.at[i]
        )
        for i in range(8)
    ]
    for load in loads:
        load.start()

    barrier = pltpu.get_barrier_semaphore()

    def greet(k, c):
        pl.semaphore_signal(barrier, inc=1, device_id=to(k), device_id_type=MESH)
        return c

    lax.fori_loop(1, DEVS, greet, 0)

    cluster = ids[...]
    o_grp, o_mem, layer = cluster & 63, (cluster >> 6) & 1, cluster >> 7
    way = 1 - 2 * core
    dz = (way * ((o_grp >> 4) - z)) & 3
    dx = (way * (((o_grp >> 2) & 3) - x)) & 3
    dy = (way * ((o_grp & 3) - y)) & 3
    dc = (o_mem - core) & 1
    place = ((dz * 32 + dx * 8 + dy * 2 + dc) * BACK) & (DEVS - 1)
    owner_is = (iota((DEVS, rows), 0) == place).astype(jnp.float32)
    owner_bf = owner_is.astype(jnp.bfloat16)
    upper = (iota((256, 256), 0) < iota((256, 256), 1)).astype(jnp.bfloat16)
    before = jnp.zeros((DEVS, 1), jnp.float32)
    ranks = []
    for i in range(rows // 256):
        block = owner_is[:, i * 256 : (i + 1) * 256]
        ahead = dot(owner_bf[:, i * 256 : (i + 1) * 256], upper) + before
        ranks.append(jnp.sum(block * ahead, axis=0, keepdims=True))
        before = before + jnp.sum(block, axis=1, keepdims=True)
    rank = jnp.concatenate(ranks, axis=1).astype(jnp.int32)
    slot = place * SLOT + rank
    rank_is = iota((DEVS, rows), 0) == rank
    tags = dot(
        owner_bf, jnp.where(rank_is, (layer + 1).astype(jnp.float32), 0.0).astype(jnp.bfloat16), NT
    )
    tag_out[...] = tags.reshape(DEVS, 1, DEVS)
    tag_in[0] = tag_out[0]

    for i in range(8):
        loads[i].wait()
        block = raw[i * part : (i + 1) * part, :]
        factor = lax.rsqrt(jnp.mean(block * block, axis=1, keepdims=True) + 1e-06) / math.sqrt(width)
        normed[i * part : (i + 1) * part, :] = (block * factor).astype(jnp.bfloat16)

    def row_copy(k, t):
        at = pl.ds(pl.multiple_of(k * SLOT, SLOT), SLOT)
        return pltpu.make_async_remote_copy(
            src_ref=send.at[at], dst_ref=recv.at[at], send_sem=send_sem, recv_sem=recv_sem.at[t],
            device_id=to(k), device_id_type=MESH,
        )

    def tag_copy(k):
        return pltpu.make_async_remote_copy(
            src_ref=tag_out.at[k], dst_ref=tag_in.at[k], send_sem=tag_sems.at[0], recv_sem=tag_sems.at[1],
            device_id=to(k), device_id_type=MESH,
        )

    def best_copy(k):
        return pltpu.make_async_remote_copy(
            src_ref=best_out.at[k], dst_ref=best_in.at[k], send_sem=best_sems.at[0], recv_sem=best_sems.at[1],
            device_id=origin(k), device_id_type=MESH,
        )

    def whole(src, dst, sems, lo, n):
        return pltpu.make_async_remote_copy(
            src_ref=src.at[pl.ds(lo, n)], dst_ref=dst.at[pl.ds(lo, n)], send_sem=sems[0], recv_sem=sems[1],
            device_id=to(1), device_id_type=MESH,
        )

    for t in range(CHUNKS):
        pick = (iota((CHUNK, rows), 0) + t * CHUNK == slot).astype(jnp.float32).astype(jnp.bfloat16)
        send[t * CHUNK : (t + 1) * CHUNK, :] = dot(pick, normed[...]).astype(jnp.bfloat16)
        if t == 0:
            recv[:SLOT, :] = send[:SLOT, :]
            pl.semaphore_wait(barrier, DEVS - 1)

        def start(k, c):
            row_copy(k, t).start()
            return c

        lax.fori_loop(max(1, t * GROUP), (t + 1) * GROUP, start, 0)
        if t == 0:

            def start_tag(k, c):
                tag_copy(k).start()
                return c

            lax.fori_loop(1, DEVS, start_tag, 0)

    whole(tag_out, tag_in, (tag_sems.at[0], tag_sems.at[1]), 1, DEVS - 1).wait()
    own_lane = iota((CHUNK, DEVS), 1) == iota((CHUNK, DEVS), 0) % SLOT
    for t in range(CHUNKS):
        spread = jnp.broadcast_to(tag_in[t * GROUP : (t + 1) * GROUP], (GROUP, SLOT, DEVS))
        tag = jnp.where(own_lane, spread.reshape(CHUNK, DEVS), 0.0).astype(jnp.bfloat16)
        tag_col[t * CHUNK : (t + 1) * CHUNK, :] = dot(tag, jnp.ones((DEVS, DEVS), jnp.bfloat16))
        along = dot(jnp.ones((8, DEVS), jnp.bfloat16), tag, NT)
        tag_row[:, t * CHUNK : (t + 1) * CHUNK] = jnp.where(along == 0.0, -1.0, along)
    col_max[...] = jnp.full(col_max.shape, -1.0, jnp.float32)

    def tile(t, j, diagonal, best):
        at_t = pl.ds(pl.multiple_of(t * CHUNK, CHUNK), CHUNK)
        at_j = pl.ds(pl.multiple_of(j * CHUNK, CHUNK), CHUNK)
        scores = dot(recv[at_t, :], recv[at_j, :], NT)
        col_tag = tag_col[at_t, :]
        row_tag = tag_row[0:1, at_j]
        allowed = jnp.concatenate([col_tag, col_tag], axis=1) == row_tag
        if diagonal:
            allowed = allowed & (iota((CHUNK, CHUNK), 0) != iota((CHUNK, CHUNK), 1))
        scores = jnp.where(allowed, scores, -1.0)
        if not diagonal:
            col_max[:, at_j] = jnp.maximum(
                col_max[:, at_j], jnp.max(scores.reshape(CHUNK // 8, 8, CHUNK), axis=0)
            )
        return jnp.maximum(best, jnp.maximum(scores[:, :128], scores[:, 128:]))

    for t in range(CHUNKS):
        lo = 1 if t == 0 else t * GROUP
        n = (t + 1) * GROUP - lo
        whole(send, recv, (send_sem, recv_sem.at[t]), lo * SLOT, n * SLOT).wait_recv()
        best = tile(t, t, True, jnp.full((CHUNK, 128), -1.0, jnp.float32))
        if t:
            best = lax.fori_loop(0, t, lambda j, b: tile(t, j, False, b), best)
        row_max[t * CHUNK : (t + 1) * CHUNK, :] = best

    eye = iota((128, 128), 0) == iota((128, 128), 1)
    for t in range(CHUNKS):
        along = jnp.max(col_max[:, t * CHUNK : (t + 1) * CHUNK], axis=0, keepdims=True)
        turned = jnp.concatenate(
            [jnp.where(eye, along[:, :128], -1.0), jnp.where(eye, along[:, 128:], -1.0)], axis=0
        )
        best = jnp.max(jnp.maximum(row_max[t * CHUNK : (t + 1) * CHUNK, :], turned), axis=1, keepdims=True)
        laid = jnp.where(own_lane, best, -1.0).reshape(GROUP, SLOT, DEVS)
        best_out[t * GROUP : (t + 1) * GROUP] = jnp.max(laid, axis=1, keepdims=True)

        def give(k, c):
            best_copy(k).start()
            return c

        lax.fori_loop(max(1, t * GROUP), (t + 1) * GROUP, give, 0)
        if t == 0:
            best_in[0] = best_out[0]

    whole(send, recv, (send_sem, recv_sem.at[0]), SLOT, (DEVS - 1) * SLOT).wait_send()
    whole(best_out, best_in, (best_sems.at[0], best_sems.at[1]), 1, DEVS - 1).wait()
    rank_bf = rank_is.astype(jnp.float32).astype(jnp.bfloat16)
    rest = best_in[...].reshape(DEVS, DEVS)
    found = jnp.zeros((DEVS, rows), jnp.float32)
    for _ in range(3):
        piece = rest.astype(jnp.bfloat16)
        rest = rest - piece.astype(jnp.float32)
        found = found + dot(piece, rank_bf)
    out[...] = jnp.sum(owner_is * found, axis=0, keepdims=True)


def body(embeddings, cluster_of):
    rows, width = embeddings.shape
    slots = DEVS * SLOT
    best = pl.pallas_call(
        kernel,
        out_shape=jax.ShapeDtypeStruct((1, rows), jnp.float32),
        in_specs=[pl.BlockSpec(memory_space=pl.ANY), pl.BlockSpec(memory_space=pltpu.VMEM)],
        out_specs=pl.BlockSpec(memory_space=pltpu.VMEM),
        scratch_shapes=[
            pltpu.VMEM((rows, width), jnp.float32),
            pltpu.VMEM((rows, width), jnp.bfloat16),
            pltpu.VMEM((slots, width), jnp.bfloat16),
            pltpu.VMEM((slots, width), jnp.bfloat16),
            pltpu.VMEM((DEVS, 1, DEVS), jnp.float32),
            pltpu.VMEM((DEVS, 1, DEVS), jnp.float32),
            pltpu.VMEM((DEVS, 1, DEVS), jnp.float32),
            pltpu.VMEM((DEVS, 1, DEVS), jnp.float32),
            pltpu.VMEM((slots, 128), jnp.float32),
            pltpu.VMEM((8, slots), jnp.float32),
            pltpu.VMEM((slots, 128), jnp.float32),
            pltpu.VMEM((8, slots), jnp.float32),
            pltpu.SemaphoreType.DMA((8,)),
            pltpu.SemaphoreType.DMA,
            pltpu.SemaphoreType.DMA((CHUNKS,)),
            pltpu.SemaphoreType.DMA((2,)),
            pltpu.SemaphoreType.DMA((2,)),
        ],
        compiler_params=pltpu.CompilerParams(
            collective_id=0, has_side_effects=True, vmem_limit_bytes=48 << 20
        ),
        cost_estimate=pl.CostEstimate(
            flops=2 * slots * slots * width, bytes_accessed=4 * rows * width, transcendentals=rows
        ),
        name="nearest",
    )(embeddings, cluster_of.reshape(1, rows))
    return best.reshape(rows)


def solution(mesh):
    return jax.shard_map(
        body,
        mesh=mesh,
        in_specs=(P(("grp", "mem"), None), P(("grp", "mem"))),
        out_specs=P(("grp", "mem")),
        check_vma=False,
    )
```

```python
import functools
import math

import jax
import jax.numpy as jnp
from jax import lax
from jax.experimental import pallas as pl
from jax.experimental.pallas import tpu as pltpu
from jax.sharding import PartitionSpec as P

MESH = pl.DeviceIdType.MESH
STEP = 115
BACK = 59
DEVS = 128
SLOT = 16
GROUP = 16
CHUNK = GROUP * SLOT
CHUNKS = DEVS // GROUP
NT = (((1,), (1,)), ((), ()))


def dot(a, b, dims=(((1,), (0,)), ((), ()))):
    return lax.dot_general(a, b, dims, preferred_element_type=jnp.float32)


def iota(shape, dim):
    return lax.broadcasted_iota(jnp.int32, shape, dim)


def kernel(
    emb, ids, out,
    raw, normed, send, recv, tag_out, tag_in, best_out, best_in,
    tag_col, tag_row, row_max, col_max,
    load_sem, send_sem, recv_sem, tag_sems, best_sems,
):
    rows, width = raw.shape
    grp, core = lax.axis_index("grp"), lax.axis_index("mem")
    z, x, y = grp >> 4, (grp >> 2) & 3, grp & 3

    def coords(k, away):
        q = (k * STEP) & (DEVS - 1)
        there = core ^ (q & 1)
        way = 1 - 2 * core if away else 2 * there - 1
        g = (
            ((z + way * (q >> 5)) & 3) * 16
            + ((x + way * ((q >> 3) & 3)) & 3) * 4
            + ((y + way * ((q >> 1) & 3)) & 3)
        )
        return g, there

    part = rows // 8
    loads = [
        pltpu.make_async_copy(
            emb.at[pl.ds(i * part, part)], raw.at[pl.ds(i * part, part)], load_sem.at[i]
        )
        for i in range(8)
    ]
    for load in loads:
        load.start()

    barrier = pltpu.get_barrier_semaphore()

    me = grp * 2 + core

    def greet(k, c):
        other = (me + k) & (DEVS - 1)
        pl.semaphore_signal(barrier, inc=1, device_id=(other >> 1, other & 1), device_id_type=MESH)
        return c

    lax.fori_loop(1, DEVS, greet, 0)

    cluster = ids[...]
    o_grp, o_mem, layer = cluster & 63, (cluster >> 6) & 1, cluster >> 7
    way = 1 - 2 * core
    dz = (way * ((o_grp >> 4) - z)) & 3
    dx = (way * (((o_grp >> 2) & 3) - x)) & 3
    dy = (way * ((o_grp & 3) - y)) & 3
    dc = (o_mem - core) & 1
    place = ((dz * 32 + dx * 8 + dy * 2 + dc) * BACK) & (DEVS - 1)
    owner_is = (iota((DEVS, rows), 0) == place).astype(jnp.float32)
    owner_bf = owner_is.astype(jnp.bfloat16)
    upper = (iota((256, 256), 0) < iota((256, 256), 1)).astype(jnp.bfloat16)
    before = jnp.zeros((DEVS, 1), jnp.float32)
    ranks = []
    for i in range(rows // 256):
        block = owner_is[:, i * 256 : (i + 1) * 256]
        ahead = dot(owner_bf[:, i * 256 : (i + 1) * 256], upper) + before
        ranks.append(jnp.sum(block * ahead, axis=0, keepdims=True))
        before = before + jnp.sum(block, axis=1, keepdims=True)
    rank = jnp.concatenate(ranks, axis=1).astype(jnp.int32)
    slot = place * SLOT + rank
    rank_is = iota((DEVS, rows), 0) == rank
    tags = dot(
        owner_bf, jnp.where(rank_is, (layer + 1).astype(jnp.float32), 0.0).astype(jnp.bfloat16), NT
    )
    tag_out[...] = tags.reshape(DEVS, 1, DEVS)
    tag_in[0] = tag_out[0]

    for i in range(8):
        loads[i].wait()
        block = raw[i * part : (i + 1) * part, :]
        factor = lax.rsqrt(jnp.mean(block * block, axis=1, keepdims=True) + 1e-06) / math.sqrt(width)
        normed[i * part : (i + 1) * part, :] = (block * factor).astype(jnp.bfloat16)

    def row_copy(k, t):
        at = pl.ds(pl.multiple_of(k * SLOT, SLOT), SLOT)
        return pltpu.make_async_remote_copy(
            src_ref=send.at[at], dst_ref=recv.at[at], send_sem=send_sem, recv_sem=recv_sem.at[t],
            device_id=coords(k, True), device_id_type=MESH,
        )

    def tag_copy(k):
        return pltpu.make_async_remote_copy(
            src_ref=tag_out.at[k], dst_ref=tag_in.at[k], send_sem=tag_sems.at[0], recv_sem=tag_sems.at[1],
            device_id=coords(k, True), device_id_type=MESH,
        )

    def best_copy(k):
        return pltpu.make_async_remote_copy(
            src_ref=best_out.at[k], dst_ref=best_in.at[k], send_sem=best_sems.at[0], recv_sem=best_sems.at[1],
            device_id=coords(k, False), device_id_type=MESH,
        )

    def whole(src, dst, sems, lo, n):
        return pltpu.make_async_remote_copy(
            src_ref=src.at[pl.ds(lo, n)], dst_ref=dst.at[pl.ds(lo, n)], send_sem=sems[0], recv_sem=sems[1],
            device_id=coords(1, True), device_id_type=MESH,
        )

    for t in range(CHUNKS):
        pick = (iota((CHUNK, rows), 0) + t * CHUNK == slot).astype(jnp.float32).astype(jnp.bfloat16)
        send[t * CHUNK : (t + 1) * CHUNK, :] = dot(pick, normed[...]).astype(jnp.bfloat16)
        if t == 0:
            recv[:SLOT, :] = send[:SLOT, :]
            pl.semaphore_wait(barrier, DEVS - 1)

        def start(k, c):
            row_copy(k, t).start()
            return c

        lax.fori_loop(max(1, t * GROUP), (t + 1) * GROUP, start, 0)
        if t == 0:

            def start_tag(k, c):
                tag_copy(k).start()
                return c

            lax.fori_loop(1, DEVS, start_tag, 0)

    whole(tag_out, tag_in, (tag_sems.at[0], tag_sems.at[1]), 1, DEVS - 1).wait()
    own_lane = iota((CHUNK, DEVS), 1) == iota((CHUNK, DEVS), 0) % SLOT
    for t in range(CHUNKS):
        spread = jnp.broadcast_to(tag_in[t * GROUP : (t + 1) * GROUP], (GROUP, SLOT, DEVS))
        tag = jnp.where(own_lane, spread.reshape(CHUNK, DEVS), 0.0).astype(jnp.bfloat16)
        tag_col[t * CHUNK : (t + 1) * CHUNK, :] = dot(tag, jnp.ones((DEVS, DEVS), jnp.bfloat16))
        along = dot(jnp.ones((8, DEVS), jnp.bfloat16), tag, NT)
        tag_row[:, t * CHUNK : (t + 1) * CHUNK] = jnp.where(along == 0.0, -1.0, along)
    col_max[...] = jnp.full(col_max.shape, -1.0, jnp.float32)

    def tile(t, j, diagonal, best):
        at_t = pl.ds(pl.multiple_of(t * CHUNK, CHUNK), CHUNK)
        at_j = pl.ds(pl.multiple_of(j * CHUNK, CHUNK), CHUNK)
        scores = dot(recv[at_t, :], recv[at_j, :], NT)
        col_tag = tag_col[at_t, :]
        row_tag = tag_row[0:1, at_j]
        allowed = jnp.concatenate([col_tag, col_tag], axis=1) == row_tag
        if diagonal:
            allowed = allowed & (iota((CHUNK, CHUNK), 0) != iota((CHUNK, CHUNK), 1))
        scores = jnp.where(allowed, scores, -1.0)
        if not diagonal:
            col_max[:, at_j] = jnp.maximum(
                col_max[:, at_j], jnp.max(scores.reshape(CHUNK // 8, 8, CHUNK), axis=0)
            )
        return jnp.maximum(best, jnp.maximum(scores[:, :128], scores[:, 128:]))

    for t in range(CHUNKS):
        lo = 1 if t == 0 else t * GROUP
        n = (t + 1) * GROUP - lo
        whole(send, recv, (send_sem, recv_sem.at[t]), lo * SLOT, n * SLOT).wait_recv()
        best = tile(t, t, True, jnp.full((CHUNK, 128), -1.0, jnp.float32))
        if t:
            best = lax.fori_loop(0, t, lambda j, b: tile(t, j, False, b), best)
        row_max[t * CHUNK : (t + 1) * CHUNK, :] = best

    eye = iota((128, 128), 0) == iota((128, 128), 1)
    for t in range(CHUNKS):
        along = jnp.max(col_max[:, t * CHUNK : (t + 1) * CHUNK], axis=0, keepdims=True)
        turned = jnp.concatenate(
            [jnp.where(eye, along[:, :128], -1.0), jnp.where(eye, along[:, 128:], -1.0)], axis=0
        )
        best = jnp.max(jnp.maximum(row_max[t * CHUNK : (t + 1) * CHUNK, :], turned), axis=1, keepdims=True)
        laid = jnp.where(own_lane, best, -1.0).reshape(GROUP, SLOT, DEVS)
        best_out[t * GROUP : (t + 1) * GROUP] = jnp.max(laid, axis=1, keepdims=True)

        def give(k, c):
            best_copy(k).start()
            return c

        lax.fori_loop(max(1, t * GROUP), (t + 1) * GROUP, give, 0)
        if t == 0:
            best_in[0] = best_out[0]

    whole(send, recv, (send_sem, recv_sem.at[0]), SLOT, (DEVS - 1) * SLOT).wait_send()
    whole(best_out, best_in, (best_sems.at[0], best_sems.at[1]), 1, DEVS - 1).wait()
    rank_bf = rank_is.astype(jnp.float32).astype(jnp.bfloat16)
    rest = best_in[...].reshape(DEVS, DEVS)
    found = jnp.zeros((DEVS, rows), jnp.float32)
    for _ in range(3):
        piece = rest.astype(jnp.bfloat16)
        rest = rest - piece.astype(jnp.float32)
        found = found + dot(piece, rank_bf)
    out[...] = jnp.sum(owner_is * found, axis=0, keepdims=True)


def body(embeddings, cluster_of):
    rows, width = embeddings.shape
    slots = DEVS * SLOT
    best = pl.pallas_call(
        kernel,
        out_shape=jax.ShapeDtypeStruct((1, rows), jnp.float32),
        in_specs=[pl.BlockSpec(memory_space=pl.ANY), pl.BlockSpec(memory_space=pltpu.VMEM)],
        out_specs=pl.BlockSpec(memory_space=pltpu.VMEM),
        scratch_shapes=[
            pltpu.VMEM((rows, width), jnp.float32),
            pltpu.VMEM((rows, width), jnp.bfloat16),
            pltpu.VMEM((slots, width), jnp.bfloat16),
            pltpu.VMEM((slots, width), jnp.bfloat16),
            pltpu.VMEM((DEVS, 1, DEVS), jnp.float32),
            pltpu.VMEM((DEVS, 1, DEVS), jnp.float32),
            pltpu.VMEM((DEVS, 1, DEVS), jnp.float32),
            pltpu.VMEM((DEVS, 1, DEVS), jnp.float32),
            pltpu.VMEM((slots, 128), jnp.float32),
            pltpu.VMEM((8, slots), jnp.float32),
            pltpu.VMEM((slots, 128), jnp.float32),
            pltpu.VMEM((8, slots), jnp.float32),
            pltpu.SemaphoreType.DMA((8,)),
            pltpu.SemaphoreType.DMA,
            pltpu.SemaphoreType.DMA((CHUNKS,)),
            pltpu.SemaphoreType.DMA((2,)),
            pltpu.SemaphoreType.DMA((2,)),
        ],
        compiler_params=pltpu.CompilerParams(
            collective_id=0, has_side_effects=True, vmem_limit_bytes=60 << 20
        ),
        cost_estimate=pl.CostEstimate(
            flops=2 * slots * slots * width, bytes_accessed=4 * rows * width, transcendentals=rows
        ),
        name="nearest",
    )(embeddings, cluster_of.reshape(1, rows))
    return best.reshape(rows)


def solution(mesh):
    return jax.shard_map(
        body,
        mesh=mesh,
        in_specs=(P(("grp", "mem"), None), P(("grp", "mem"))),
        out_specs=P(("grp", "mem")),
        check_vma=False,
    )
```

```python
import functools
import math

import jax
import jax.numpy as jnp
from jax import lax
from jax.experimental import pallas as pl
from jax.experimental.pallas import tpu as pltpu
from jax.sharding import PartitionSpec as P

MESH = pl.DeviceIdType.MESH
STEP = 115
BACK = 59
DEVS = 128
SLOT = 16
GROUP = 16
CHUNK = GROUP * SLOT
CHUNKS = DEVS // GROUP
NT = (((1,), (1,)), ((), ()))


def dot(a, b, dims=(((1,), (0,)), ((), ()))):
    return lax.dot_general(a, b, dims, preferred_element_type=jnp.float32)


def iota(shape, dim):
    return lax.broadcasted_iota(jnp.int32, shape, dim)


def kernel(
    emb, ids_in, out,
    raw, normed, send, recv, tag_out, tag_in, best_out, best_in,
    tag_col, tag_row, row_max, col_max, ids,
    load_sem, send_sem, recv_sem, tag_sems, best_sems,
):
    rows, width = raw.shape
    grp, core = lax.axis_index("grp"), lax.axis_index("mem")
    z, x, y = grp >> 4, (grp >> 2) & 3, grp & 3

    def lines(way):
        return [
            [((base + way * d) & 3) * scale for d in range(4)]
            for base, scale in ((z, 16), (x, 4), (y, 1))
        ]

    aways = lines(1 - 2 * core)
    homes = [lines(2 * core - 1), aways]

    def away(k):
        q = (k * STEP) & (DEVS - 1)
        zs, xs, ys = aways
        return zs[q >> 5] + xs[(q >> 3) & 3] + ys[(q >> 1) & 3], core ^ (q & 1)

    def home(k):
        q = (k * STEP) & (DEVS - 1)
        zs, xs, ys = homes[q & 1]
        return zs[q >> 5] + xs[(q >> 3) & 3] + ys[(q >> 1) & 3], core ^ (q & 1)

    part = rows // 8
    loads = [
        pltpu.make_async_copy(
            emb.at[pl.ds(i * part, part)], raw.at[pl.ds(i * part, part)], load_sem.at[i]
        )
        for i in range(8)
    ]
    ids_load = pltpu.make_async_copy(ids_in, ids, load_sem.at[8])
    ids_load.start()
    for load in loads:
        load.start()

    barrier = pltpu.get_barrier_semaphore()

    me = grp * 2 + core

    def greet(lo, hi):
        for k in range(lo, hi):
            other = (me + k) & (DEVS - 1)
            pl.semaphore_signal(
                barrier, inc=1, device_id=(other >> 1, other & 1), device_id_type=MESH
            )

    greet(1, DEVS)

    ids_load.wait()
    cluster = ids[...]
    o_grp, o_mem, layer = cluster & 63, (cluster >> 6) & 1, cluster >> 7
    way = 1 - 2 * core
    dz = (way * ((o_grp >> 4) - z)) & 3
    dx = (way * (((o_grp >> 2) & 3) - x)) & 3
    dy = (way * ((o_grp & 3) - y)) & 3
    dc = (o_mem - core) & 1
    place = ((dz * 32 + dx * 8 + dy * 2 + dc) * BACK) & (DEVS - 1)
    owner_is = (iota((DEVS, rows), 0) == place).astype(jnp.float32)
    owner_bf = owner_is.astype(jnp.bfloat16)
    upper = (iota((256, 256), 0) < iota((256, 256), 1)).astype(jnp.bfloat16)
    before = jnp.zeros((DEVS, 1), jnp.float32)
    ranks = []
    for i in range(rows // 256):
        block = owner_is[:, i * 256 : (i + 1) * 256]
        ahead = dot(owner_bf[:, i * 256 : (i + 1) * 256], upper) + before
        ranks.append(jnp.sum(block * ahead, axis=0, keepdims=True))
        before = before + jnp.sum(block, axis=1, keepdims=True)
    rank = jnp.concatenate(ranks, axis=1).astype(jnp.int32)
    slot = place * SLOT + rank
    rank_is = iota((DEVS, rows), 0) == rank
    tags = dot(
        owner_bf, jnp.where(rank_is, (layer + 1).astype(jnp.float32), 0.0).astype(jnp.bfloat16), NT
    )
    tag_out[...] = tags.reshape(DEVS, 1, DEVS)
    tag_in[0] = tag_out[0]

    for i in range(8):
        loads[i].wait()
        block = raw[i * part : (i + 1) * part, :]
        factor = lax.rsqrt(jnp.mean(block * block, axis=1, keepdims=True) + 1e-06) / math.sqrt(width)
        normed[i * part : (i + 1) * part, :] = (block * factor).astype(jnp.bfloat16)

    def row_copy(k, t):
        at = pl.ds(k * SLOT, SLOT)
        return pltpu.make_async_remote_copy(
            src_ref=send.at[at], dst_ref=recv.at[at], send_sem=send_sem, recv_sem=recv_sem.at[t],
            device_id=away(k), device_id_type=MESH,
        )

    def tag_copy(k):
        return pltpu.make_async_remote_copy(
            src_ref=tag_out.at[k], dst_ref=tag_in.at[k], send_sem=tag_sems.at[0], recv_sem=tag_sems.at[1],
            device_id=away(k), device_id_type=MESH,
        )

    def best_copy(k):
        return pltpu.make_async_remote_copy(
            src_ref=best_out.at[k], dst_ref=best_in.at[k], send_sem=best_sems.at[0], recv_sem=best_sems.at[1],
            device_id=home(k), device_id_type=MESH,
        )

    def whole(src, dst, sems, lo, n):
        return pltpu.make_async_remote_copy(
            src_ref=src.at[pl.ds(lo, n)], dst_ref=dst.at[pl.ds(lo, n)], send_sem=sems[0], recv_sem=sems[1],
            device_id=away(1), device_id_type=MESH,
        )

    for t in range(CHUNKS):
        pick = (iota((CHUNK, rows), 0) + t * CHUNK == slot).astype(jnp.float32).astype(jnp.bfloat16)
        send[t * CHUNK : (t + 1) * CHUNK, :] = dot(pick, normed[...]).astype(jnp.bfloat16)
        if t == 0:
            recv[:SLOT, :] = send[:SLOT, :]
            pl.semaphore_wait(barrier, DEVS - 1)

        for k in range(max(1, t * GROUP), (t + 1) * GROUP):
            row_copy(k, t).start()
        if t == 0:
            for k in range(1, DEVS):
                tag_copy(k).start()

    whole(tag_out, tag_in, (tag_sems.at[0], tag_sems.at[1]), 1, DEVS - 1).wait()
    own_lane = iota((CHUNK, DEVS), 1) == iota((CHUNK, DEVS), 0) % SLOT
    for t in range(CHUNKS):
        spread = jnp.broadcast_to(tag_in[t * GROUP : (t + 1) * GROUP], (GROUP, SLOT, DEVS))
        tag = jnp.where(own_lane, spread.reshape(CHUNK, DEVS), 0.0).astype(jnp.bfloat16)
        tag_col[t * CHUNK : (t + 1) * CHUNK, :] = dot(tag, jnp.ones((DEVS, DEVS), jnp.bfloat16))
        along = dot(jnp.ones((8, DEVS), jnp.bfloat16), tag, NT)
        tag_row[:, t * CHUNK : (t + 1) * CHUNK] = jnp.where(along == 0.0, -1.0, along)

    row_max[...] = jnp.full(row_max.shape, -1.0, jnp.float32)

    def meet(t, lo, n, diagonal):
        own = recv[t * CHUNK : (t + 1) * CHUNK, :]
        scores = dot(recv[lo : lo + n, :], own, NT)
        tags = tag_col[lo : lo + n, :]
        allowed = jnp.concatenate([tags, tags], axis=1) == tag_row[0:1, t * CHUNK : (t + 1) * CHUNK]
        if diagonal:
            allowed = allowed & (iota((n, CHUNK), 0) != iota((n, CHUNK), 1))
        scores = jnp.where(allowed, scores, -1.0)
        row_max[lo : lo + n, :] = jnp.maximum(
            row_max[lo : lo + n, :], jnp.maximum(scores[:, :128], scores[:, 128:])
        )
        if diagonal:
            return jnp.full((8, CHUNK), -1.0, jnp.float32)
        return jnp.max(scores.reshape(n // 8, 8, CHUNK), axis=0)

    for t in range(CHUNKS):
        lo = 1 if t == 0 else t * GROUP
        n = (t + 1) * GROUP - lo
        whole(send, recv, (send_sem, recv_sem.at[t]), lo * SLOT, n * SLOT).wait_recv()
        best = meet(t, t * CHUNK, CHUNK, True)
        for at in range(0, t * CHUNK, 512):
            best = jnp.maximum(best, meet(t, at, min(512, t * CHUNK - at), False))
        col_max[:, t * CHUNK : (t + 1) * CHUNK] = best

    eye = iota((128, 128), 0) == iota((128, 128), 1)
    for t in range(CHUNKS):
        along = jnp.max(col_max[:, t * CHUNK : (t + 1) * CHUNK], axis=0, keepdims=True)
        turned = jnp.concatenate(
            [jnp.where(eye, along[:, :128], -1.0), jnp.where(eye, along[:, 128:], -1.0)], axis=0
        )
        best = jnp.max(jnp.maximum(row_max[t * CHUNK : (t + 1) * CHUNK, :], turned), axis=1, keepdims=True)
        laid = jnp.where(own_lane, best, -1.0).reshape(GROUP, SLOT, DEVS)
        best_out[t * GROUP : (t + 1) * GROUP] = jnp.max(laid, axis=1, keepdims=True)

        for k in range(max(1, t * GROUP), (t + 1) * GROUP):
            best_copy(k).start()
        if t == 0:
            best_in[0] = best_out[0]

    whole(send, recv, (send_sem, recv_sem.at[0]), SLOT, (DEVS - 1) * SLOT).wait_send()
    whole(best_out, best_in, (best_sems.at[0], best_sems.at[1]), 1, DEVS - 1).wait()
    rank_bf = rank_is.astype(jnp.float32).astype(jnp.bfloat16)
    rest = best_in[...].reshape(DEVS, DEVS)
    found = jnp.zeros((DEVS, rows), jnp.float32)
    for _ in range(3):
        piece = rest.astype(jnp.bfloat16)
        rest = rest - piece.astype(jnp.float32)
        found = found + dot(piece, rank_bf)
    out[...] = jnp.sum(owner_is * found, axis=0, keepdims=True)


def body(embeddings, cluster_of):
    rows, width = embeddings.shape
    slots = DEVS * SLOT
    best = pl.pallas_call(
        kernel,
        out_shape=jax.ShapeDtypeStruct((1, rows), jnp.float32),
        in_specs=[pl.BlockSpec(memory_space=pl.ANY), pl.BlockSpec(memory_space=pl.ANY)],
        out_specs=pl.BlockSpec(memory_space=pltpu.VMEM),
        scratch_shapes=[
            pltpu.VMEM((rows, width), jnp.float32),
            pltpu.VMEM((rows, width), jnp.bfloat16),
            pltpu.VMEM((slots, width), jnp.bfloat16),
            pltpu.VMEM((slots, width), jnp.bfloat16),
            pltpu.VMEM((DEVS, 1, DEVS), jnp.float32),
            pltpu.VMEM((DEVS, 1, DEVS), jnp.float32),
            pltpu.VMEM((DEVS, 1, DEVS), jnp.float32),
            pltpu.VMEM((DEVS, 1, DEVS), jnp.float32),
            pltpu.VMEM((slots, 128), jnp.float32),
            pltpu.VMEM((8, slots), jnp.float32),
            pltpu.VMEM((slots, 128), jnp.float32),
            pltpu.VMEM((8, slots), jnp.float32),
            pltpu.VMEM((1, rows), jnp.int32),
            pltpu.SemaphoreType.DMA((9,)),
            pltpu.SemaphoreType.DMA,
            pltpu.SemaphoreType.DMA((CHUNKS,)),
            pltpu.SemaphoreType.DMA((2,)),
            pltpu.SemaphoreType.DMA((2,)),
        ],
        compiler_params=pltpu.CompilerParams(
            collective_id=0, has_side_effects=True, vmem_limit_bytes=60 << 20
        ),
        cost_estimate=pl.CostEstimate(
            flops=2 * slots * slots * width, bytes_accessed=4 * rows * width, transcendentals=rows
        ),
        name="nearest",
    )(embeddings, cluster_of.reshape(1, rows))
    return best.reshape(rows)


def solution(mesh):
    return jax.shard_map(
        body,
        mesh=mesh,
        in_specs=(P(("grp", "mem"), None), P(("grp", "mem"))),
        out_specs=P(("grp", "mem")),
        check_vma=False,
    )
```

```python
import functools
import math

import jax
import jax.numpy as jnp
from jax import lax
from jax.experimental import pallas as pl
from jax.experimental.pallas import tpu as pltpu
from jax.sharding import PartitionSpec as P

MESH = pl.DeviceIdType.MESH
DEVS = 128


def axes(q):
    return (q >> 5 != 0) + ((q >> 3) & 3 != 0) + ((q >> 1) & 3 != 0)


LCG = [(115 * k) % DEVS for k in range(DEVS)]
def spread(a, b):
    n = len(a) + len(b)
    out, i = [], 0
    for k in range(n):
        if (k + 1) * len(a) // n > i:
            out.append(a[i])
            i += 1
        else:
            out.append(b[k - i])
    return out


ONE, TWO, THREE = ([q for q in LCG if q and max(1, axes(q)) == n] for n in (1, 2, 3))
ORDER = [0] + ONE + TWO[:24] + spread(TWO[24:], THREE)
SLOT = 16
GROUP = 16
CHUNK = GROUP * SLOT
CHUNKS = DEVS // GROUP
NT = (((1,), (1,)), ((), ()))


def dot(a, b, dims=(((1,), (0,)), ((), ()))):
    return lax.dot_general(a, b, dims, preferred_element_type=jnp.float32)


def iota(shape, dim):
    return lax.broadcasted_iota(jnp.int32, shape, dim)


def kernel(
    emb, ids_in, order_in, order_row_in, out,
    raw, normed, send, recv, tag_out, tag_in, best_out, best_in,
    tag_col, tag_row, row_max, col_max, ids, order, order_row, laid,
    load_sem, send_sem, recv_sem, tag_sems, best_sems, entry_sems,
):
    rows, width = raw.shape
    grp, core = lax.axis_index("grp"), lax.axis_index("mem")
    z, x, y = grp >> 4, (grp >> 2) & 3, grp & 3

    def lines(way):
        return [
            [((base + way * d) & 3) * scale for d in range(4)]
            for base, scale in ((z, 16), (x, 4), (y, 1))
        ]

    aways = lines(1 - 2 * core)
    aways = lines(1 - 2 * core)
    me = grp * 2 + core

    def away(k):
        q = ORDER[k]
        zs, xs, ys = aways
        return zs[q >> 5] + xs[(q >> 3) & 3] + ys[(q >> 1) & 3], core ^ (q & 1)

    part = rows // 8
    loads = [
        pltpu.make_async_copy(
            emb.at[pl.ds(i * part, part)], raw.at[pl.ds(i * part, part)], load_sem.at[i]
        )
        for i in range(8)
    ]
    ids_load = pltpu.make_async_copy(ids_in, ids, load_sem.at[8])
    ids_load.start()
    order_load = pltpu.make_async_copy(order_in, order, load_sem.at[9])
    order_load.start()
    row_load = pltpu.make_async_copy(order_row_in, order_row, load_sem.at[10])
    row_load.start()
    for load in loads:
        load.start()

    barrier = pltpu.get_barrier_semaphore()

    def greet(sem, other):
        pl.semaphore_signal(sem, inc=1, device_id=other, device_id_type=MESH)

    zs, xs, ys = aways
    z_line = [zs[d] + xs[0] + ys[0] for d in range(1, 4)]
    x_line = [zs[0] + xs[d] + ys[0] for d in range(1, 4)]
    y_line = [zs[0] + xs[0] + ys[d] for d in range(1, 4)]
    greet(barrier, (grp, core ^ 1))
    for chip in z_line + x_line + y_line:
        greet(barrier, (chip, core))
        greet(barrier, (chip, core ^ 1))

    def enter(stage):
        if stage == 1:
            pl.semaphore_wait(barrier, 19)
            for chip in z_line + x_line + y_line:
                greet(entry_sems.at[0], (chip, core))
        elif stage == 2:
            pl.semaphore_wait(entry_sems.at[0], 9)
            for chip in z_line:
                greet(entry_sems.at[1], (chip, core))
        else:
            pl.semaphore_wait(entry_sems.at[1], 3)

    ids_load.wait()
    cluster = ids[...]
    o_grp, o_mem, layer = cluster & 63, (cluster >> 6) & 1, cluster >> 7
    way = 1 - 2 * core
    dz = (way * ((o_grp >> 4) - z)) & 3
    dx = (way * (((o_grp >> 2) & 3) - x)) & 3
    dy = (way * ((o_grp & 3) - y)) & 3
    dc = (o_mem - core) & 1
    order_load.wait()
    row_load.wait()
    shift = order_row[...]
    there = core ^ (shift & 1)
    back = 2 * there - 1
    source = (
        ((z + back * (shift >> 5)) & 3) * 32
        + ((x + back * ((shift >> 3) & 3)) & 3) * 8
        + ((y + back * ((shift >> 1) & 3)) & 3) * 2
        + there
    )
    to_source = (iota((DEVS, DEVS), 0) == source).astype(jnp.float32).astype(jnp.bfloat16)
    owner_is = (order[...] == dz * 32 + dx * 8 + dy * 2 + dc).astype(jnp.float32)
    owner_bf = owner_is.astype(jnp.bfloat16)
    upper = (iota((256, 256), 0) < iota((256, 256), 1)).astype(jnp.bfloat16)
    before = (iota((DEVS, 1), 0) * SLOT).astype(jnp.float32)
    slots = []
    for i in range(rows // 256):
        block = owner_is[:, i * 256 : (i + 1) * 256]
        ahead = dot(owner_bf[:, i * 256 : (i + 1) * 256], upper) + before
        slots.append(jnp.sum(block * ahead, axis=0, keepdims=True))
        before = before + jnp.sum(block, axis=1, keepdims=True)
    slot = jnp.concatenate(slots, axis=1).astype(jnp.int32)
    rank = slot & (SLOT - 1)
    rank_is = iota((DEVS, rows), 0) == rank
    tags = dot(
        owner_bf, jnp.where(rank_is, (layer + 1).astype(jnp.float32), 0.0).astype(jnp.bfloat16), NT
    )
    tag_out[...] = tags.reshape(DEVS, 1, DEVS)
    tag_in[0] = tag_out[0]

    for i in range(8):
        loads[i].wait()
        block = raw[i * part : (i + 1) * part, :]
        factor = lax.rsqrt(jnp.mean(block * block, axis=1, keepdims=True) + 1e-06) / math.sqrt(width)
        normed[i * part : (i + 1) * part, :] = (block * factor).astype(jnp.bfloat16)

    def row_copy(k, t):
        at = pl.ds(k * SLOT, SLOT)
        return pltpu.make_async_remote_copy(
            src_ref=send.at[at], dst_ref=recv.at[at], send_sem=send_sem, recv_sem=recv_sem.at[t],
            device_id=away(k), device_id_type=MESH,
        )

    def tag_copy(k):
        return pltpu.make_async_remote_copy(
            src_ref=tag_out.at[k], dst_ref=tag_in.at[k], send_sem=tag_sems.at[0], recv_sem=tag_sems.at[1 + k // GROUP],
            device_id=away(k), device_id_type=MESH,
        )

    def best_copy(plane, dx, dy, dc):
        chip, there = plane * 16 + xs[dx] + ys[dy], core ^ dc
        return pltpu.make_async_remote_copy(
            src_ref=best_out.at[chip * 2 + there], dst_ref=best_in.at[me],
            send_sem=best_sems.at[0], recv_sem=best_sems.at[1],
            device_id=(chip, there), device_id_type=MESH,
        )

    def whole(src, dst, sems, lo, n):
        return pltpu.make_async_remote_copy(
            src_ref=src.at[pl.ds(lo, n)], dst_ref=dst.at[pl.ds(lo, n)], send_sem=sems[0], recv_sem=sems[1],
            device_id=away(1), device_id_type=MESH,
        )

    stage = 0
    for t in range(CHUNKS):
        pick = (iota((CHUNK, rows), 0) + t * CHUNK == slot).astype(jnp.float32).astype(jnp.bfloat16)
        send[t * CHUNK : (t + 1) * CHUNK, :] = dot(pick, normed[...]).astype(jnp.bfloat16)
        if t == 0:
            recv[:SLOT, :] = send[:SLOT, :]
        for k in range(max(1, t * GROUP), (t + 1) * GROUP):
            need = max(1, axes(ORDER[k]))
            while stage < need:
                stage += 1
                enter(stage)
            tag_copy(k).start()
            row_copy(k, t).start()

    own_lane = iota((CHUNK, DEVS), 1) == iota((CHUNK, DEVS), 0) % SLOT
    row_max[...] = jnp.full(row_max.shape, -1.0, jnp.float32)

    def meet(t, lo, n, diagonal):
        own = recv[t * CHUNK : (t + 1) * CHUNK, :]
        scores = dot(recv[lo : lo + n, :], own, NT)
        tags = tag_col[lo : lo + n, :]
        allowed = jnp.concatenate([tags, tags], axis=1) == tag_row[0:1, t * CHUNK : (t + 1) * CHUNK]
        if diagonal:
            allowed = allowed & (iota((n, CHUNK), 0) != iota((n, CHUNK), 1))
        scores = jnp.where(allowed, scores, -1.0)
        row_max[lo : lo + n, :] = jnp.maximum(
            row_max[lo : lo + n, :], jnp.maximum(scores[:, :128], scores[:, 128:])
        )
        if diagonal:
            return jnp.full((8, CHUNK), -1.0, jnp.float32)
        return jnp.max(scores.reshape(n // 8, 8, CHUNK), axis=0)

    for t in range(CHUNKS):
        lo = 1 if t == 0 else t * GROUP
        n = (t + 1) * GROUP - lo
        whole(send, recv, (send_sem, recv_sem.at[t]), lo * SLOT, n * SLOT).wait_recv()
        whole(tag_out, tag_in, (tag_sems.at[0], tag_sems.at[1 + t]), lo, n).wait_recv()
        spread_tag = jnp.broadcast_to(tag_in[t * GROUP : (t + 1) * GROUP], (GROUP, SLOT, DEVS))
        tag = jnp.where(own_lane, spread_tag.reshape(CHUNK, DEVS), 0.0).astype(jnp.bfloat16)
        tag_col[t * CHUNK : (t + 1) * CHUNK, :] = dot(tag, jnp.ones((DEVS, DEVS), jnp.bfloat16))
        along = dot(jnp.ones((8, DEVS), jnp.bfloat16), tag, NT)
        tag_row[:, t * CHUNK : (t + 1) * CHUNK] = jnp.where(along == 0.0, -1.0, along)
        best = meet(t, t * CHUNK, CHUNK, True)
        for at in range(0, t * CHUNK, 512):
            best = jnp.maximum(best, meet(t, at, min(512, t * CHUNK - at), False))
        col_max[:, t * CHUNK : (t + 1) * CHUNK] = best

    eye = iota((128, 128), 0) == iota((128, 128), 1)
    for t in range(CHUNKS):
        along = jnp.max(col_max[:, t * CHUNK : (t + 1) * CHUNK], axis=0, keepdims=True)
        turned = jnp.concatenate(
            [jnp.where(eye, along[:, :128], -1.0), jnp.where(eye, along[:, 128:], -1.0)], axis=0
        )
        best = jnp.max(jnp.maximum(row_max[t * CHUNK : (t + 1) * CHUNK, :], turned), axis=1, keepdims=True)
        blocks = jnp.where(own_lane, best, -1.0).reshape(GROUP, SLOT, DEVS)
        laid[t * GROUP : (t + 1) * GROUP, :] = jnp.max(blocks, axis=1)

    def exact(rest, pick):
        total = None
        for _ in range(3):
            piece = rest.astype(jnp.bfloat16)
            rest = rest - piece.astype(jnp.float32)
            term = pick(piece)
            total = term if total is None else total + term
        return total

    best_out[...] = exact(laid[...], lambda piece: dot(to_source, piece)).reshape(DEVS, 1, DEVS)
    best_in[me] = best_out[me]
    for plane in range(4):
        for step in range(32):
            if step == 0:

                @pl.when(plane != z)
                def _():
                    best_copy(plane, 0, 0, 0).start()

            else:
                best_copy(plane, step >> 3, (step >> 1) & 3, step & 1).start()

    whole(send, recv, (send_sem, recv_sem.at[0]), SLOT, (DEVS - 1) * SLOT).wait_send()
    whole(tag_out, tag_in, (tag_sems.at[0], tag_sems.at[1]), 1, DEVS - 1).wait_send()
    whole(best_out, best_in, (best_sems.at[0], best_sems.at[1]), 1, DEVS - 1).wait()
    rank_bf = rank_is.astype(jnp.float32).astype(jnp.bfloat16)
    found = exact(best_in[...].reshape(DEVS, DEVS), lambda piece: dot(piece, rank_bf))
    owner = o_grp * 2 + o_mem
    out[...] = jnp.sum(jnp.where(iota((DEVS, rows), 0) == owner, found, 0.0), axis=0, keepdims=True)


def body(embeddings, cluster_of):
    rows, width = embeddings.shape
    slots = DEVS * SLOT
    order = jnp.array(ORDER, jnp.int32)
    best = pl.pallas_call(
        kernel,
        out_shape=jax.ShapeDtypeStruct((1, rows), jnp.float32),
        in_specs=[pl.BlockSpec(memory_space=pl.ANY)] * 4,
        out_specs=pl.BlockSpec(memory_space=pltpu.VMEM),
        scratch_shapes=[
            pltpu.VMEM((rows, width), jnp.float32),
            pltpu.VMEM((rows, width), jnp.bfloat16),
            pltpu.VMEM((slots, width), jnp.bfloat16),
            pltpu.VMEM((slots, width), jnp.bfloat16),
            pltpu.VMEM((DEVS, 1, DEVS), jnp.float32),
            pltpu.VMEM((DEVS, 1, DEVS), jnp.float32),
            pltpu.VMEM((DEVS, 1, DEVS), jnp.float32),
            pltpu.VMEM((DEVS, 1, DEVS), jnp.float32),
            pltpu.VMEM((slots, 128), jnp.float32),
            pltpu.VMEM((8, slots), jnp.float32),
            pltpu.VMEM((slots, 128), jnp.float32),
            pltpu.VMEM((8, slots), jnp.float32),
            pltpu.VMEM((1, rows), jnp.int32),
            pltpu.VMEM((DEVS, 1), jnp.int32),
            pltpu.VMEM((1, DEVS), jnp.int32),
            pltpu.VMEM((DEVS, DEVS), jnp.float32),
            pltpu.SemaphoreType.DMA((11,)),
            pltpu.SemaphoreType.DMA,
            pltpu.SemaphoreType.DMA((CHUNKS,)),
            pltpu.SemaphoreType.DMA((1 + CHUNKS,)),
            pltpu.SemaphoreType.DMA((2,)),
            pltpu.SemaphoreType.REGULAR((2,)),
        ],
        compiler_params=pltpu.CompilerParams(
            collective_id=0, has_side_effects=True, vmem_limit_bytes=60 << 20
        ),
        cost_estimate=pl.CostEstimate(
            flops=2 * slots * slots * width, bytes_accessed=4 * rows * width, transcendentals=rows
        ),
        name="nearest",
    )(embeddings, cluster_of.reshape(1, rows), order.reshape(DEVS, 1), order.reshape(1, DEVS))
    return best.reshape(rows)


def solution(mesh):
    return jax.shard_map(
        body,
        mesh=mesh,
        in_specs=(P(("grp", "mem"), None), P(("grp", "mem"))),
        out_specs=P(("grp", "mem")),
        check_vma=False,
    )
```

```python
import functools
import math

import jax
import jax.numpy as jnp
from jax import lax
from jax.experimental import pallas as pl
from jax.experimental.pallas import tpu as pltpu
from jax.sharding import PartitionSpec as P

MESH = pl.DeviceIdType.MESH
DEVS = 128


def axes(q):
    return (q >> 5 != 0) + ((q >> 3) & 3 != 0) + ((q >> 1) & 3 != 0)


LCG = [(107 * k) % DEVS for k in range(DEVS)]
def spread(a, b):
    n = len(a) + len(b)
    out, i = [], 0
    for k in range(n):
        if (k + 1) * len(a) // n > i:
            out.append(a[i])
            i += 1
        else:
            out.append(b[k - i])
    return out


ONE, TWO, THREE = ([q for q in LCG if q and max(1, axes(q)) == n] for n in (1, 2, 3))
ORDER = [0] + ONE + TWO[:24] + spread(TWO[24:], THREE)
SLOT = 16
GROUP = 16
CHUNK = GROUP * SLOT
CHUNKS = DEVS // GROUP
NT = (((1,), (1,)), ((), ()))


def dot(a, b, dims=(((1,), (0,)), ((), ()))):
    return lax.dot_general(a, b, dims, preferred_element_type=jnp.float32)


def iota(shape, dim):
    return lax.broadcasted_iota(jnp.int32, shape, dim)


def kernel(
    emb, ids_in, out,
    raw, normed, send, recv, tag_out, tag_in, best_out, best_in,
    tag_col, tag_row, row_max, col_max, ids, laid,
    load_sem, send_sem, recv_sem, tag_sems, best_sems, entry_sems,
):
    rows, width = raw.shape
    grp, core = lax.axis_index("grp"), lax.axis_index("mem")
    z, x, y = grp >> 4, (grp >> 2) & 3, grp & 3

    def lines(way):
        return [
            [((base + way * d) & 3) * scale for d in range(4)]
            for base, scale in ((z, 16), (x, 4), (y, 1))
        ]

    aways = lines(1 - 2 * core)
    aways = lines(1 - 2 * core)
    me = grp * 2 + core

    def away(k):
        q = ORDER[k]
        zs, xs, ys = aways
        return zs[q >> 5] + xs[(q >> 3) & 3] + ys[(q >> 1) & 3], core ^ (q & 1)

    part = rows // 8
    loads = [
        pltpu.make_async_copy(
            emb.at[pl.ds(i * part, part)], raw.at[pl.ds(i * part, part)], load_sem.at[i]
        )
        for i in range(8)
    ]
    ids_load = pltpu.make_async_copy(ids_in, ids, load_sem.at[8])
    ids_load.start()
    for load in loads:
        load.start()

    barrier = pltpu.get_barrier_semaphore()

    def greet(sem, other):
        pl.semaphore_signal(sem, inc=1, device_id=other, device_id_type=MESH)

    zs, xs, ys = aways
    z_line = [zs[d] + xs[0] + ys[0] for d in range(1, 4)]
    x_line = [zs[0] + xs[d] + ys[0] for d in range(1, 4)]
    y_line = [zs[0] + xs[0] + ys[d] for d in range(1, 4)]
    greet(barrier, (grp, core ^ 1))
    for chip in z_line + x_line + y_line:
        greet(barrier, (chip, core))
        greet(barrier, (chip, core ^ 1))

    def enter(stage):
        if stage == 1:
            pl.semaphore_wait(barrier, 19)
            for chip in z_line + x_line + y_line:
                greet(entry_sems.at[0], (chip, core))
        elif stage == 2:
            pl.semaphore_wait(entry_sems.at[0], 9)
            for chip in z_line:
                greet(entry_sems.at[1], (chip, core))
        else:
            pl.semaphore_wait(entry_sems.at[1], 3)

    lane = iota((1, DEVS), 1)
    parts = []
    for first in range(0, DEVS, 16):
        part_of = jnp.zeros((1, DEVS), jnp.int32)
        for k in range(first, first + 16):
            part_of = jnp.where(lane == k, ORDER[k], part_of)
        parts.append(part_of)
    shift = functools.reduce(jnp.add, parts)
    order = jnp.sum(
        jnp.where(iota((DEVS, DEVS), 0) == iota((DEVS, DEVS), 1), shift, 0).astype(jnp.float32),
        axis=1, keepdims=True,
    ).astype(jnp.int32)
    ids_load.wait()
    cluster = ids[...]
    o_grp, o_mem, layer = cluster & 63, (cluster >> 6) & 1, cluster >> 7
    way = 1 - 2 * core
    dz = (way * ((o_grp >> 4) - z)) & 3
    dx = (way * (((o_grp >> 2) & 3) - x)) & 3
    dy = (way * ((o_grp & 3) - y)) & 3
    dc = (o_mem - core) & 1
    there = core ^ (shift & 1)
    back = 2 * there - 1
    source = (
        ((z + back * (shift >> 5)) & 3) * 32
        + ((x + back * ((shift >> 3) & 3)) & 3) * 8
        + ((y + back * ((shift >> 1) & 3)) & 3) * 2
        + there
    )
    to_source = (iota((DEVS, DEVS), 0) == source).astype(jnp.float32).astype(jnp.bfloat16)
    owner_is = (order == dz * 32 + dx * 8 + dy * 2 + dc).astype(jnp.float32)
    owner_bf = owner_is.astype(jnp.bfloat16)
    upper = (iota((256, 256), 0) < iota((256, 256), 1)).astype(jnp.bfloat16)
    before = (iota((DEVS, 1), 0) * SLOT).astype(jnp.float32)
    slots = []
    for i in range(rows // 256):
        block = owner_is[:, i * 256 : (i + 1) * 256]
        ahead = dot(owner_bf[:, i * 256 : (i + 1) * 256], upper) + before
        slots.append(jnp.sum(block * ahead, axis=0, keepdims=True))
        before = before + jnp.sum(block, axis=1, keepdims=True)
    slot = jnp.concatenate(slots, axis=1).astype(jnp.int32)
    rank = slot & (SLOT - 1)
    rank_is = iota((DEVS, rows), 0) == rank
    tags = dot(
        owner_bf, jnp.where(rank_is, (layer + 1).astype(jnp.float32), 0.0).astype(jnp.bfloat16), NT
    )
    tag_out[...] = tags.reshape(DEVS, 1, DEVS)
    tag_in[0] = tag_out[0]

    for i in range(8):
        loads[i].wait()
        block = raw[i * part : (i + 1) * part, :]
        factor = lax.rsqrt(jnp.mean(block * block, axis=1, keepdims=True) + 1e-06) / math.sqrt(width)
        normed[i * part : (i + 1) * part, :] = (block * factor).astype(jnp.bfloat16)

    def row_copy(k, t):
        at = pl.ds(k * SLOT, SLOT)
        return pltpu.make_async_remote_copy(
            src_ref=send.at[at], dst_ref=recv.at[at], send_sem=send_sem, recv_sem=recv_sem.at[t],
            device_id=away(k), device_id_type=MESH,
        )

    def tag_copy(k):
        return pltpu.make_async_remote_copy(
            src_ref=tag_out.at[k], dst_ref=tag_in.at[k], send_sem=tag_sems.at[0], recv_sem=tag_sems.at[1 + k // GROUP],
            device_id=away(k), device_id_type=MESH,
        )

    def best_copy(plane, dx, dy, dc):
        chip, there = plane * 16 + xs[dx] + ys[dy], core ^ dc
        return pltpu.make_async_remote_copy(
            src_ref=best_out.at[chip * 2 + there], dst_ref=best_in.at[me],
            send_sem=best_sems.at[0], recv_sem=best_sems.at[1],
            device_id=(chip, there), device_id_type=MESH,
        )

    def whole(src, dst, sems, lo, n):
        return pltpu.make_async_remote_copy(
            src_ref=src.at[pl.ds(lo, n)], dst_ref=dst.at[pl.ds(lo, n)], send_sem=sems[0], recv_sem=sems[1],
            device_id=away(1), device_id_type=MESH,
        )

    stage = 0
    for t in range(CHUNKS):
        pick = (iota((CHUNK, rows), 0) + t * CHUNK == slot).astype(jnp.float32).astype(jnp.bfloat16)
        send[t * CHUNK : (t + 1) * CHUNK, :] = dot(pick, normed[...]).astype(jnp.bfloat16)
        if t == 0:
            recv[:SLOT, :] = send[:SLOT, :]
        for k in range(max(1, t * GROUP), (t + 1) * GROUP):
            need = max(1, axes(ORDER[k]))
            while stage < need:
                stage += 1
                enter(stage)
            tag_copy(k).start()
            row_copy(k, t).start()

    own_lane = iota((CHUNK, DEVS), 1) == iota((CHUNK, DEVS), 0) % SLOT
    row_max[...] = jnp.full(row_max.shape, -1.0, jnp.float32)

    def meet(t, lo, n, diagonal):
        own = recv[t * CHUNK : (t + 1) * CHUNK, :]
        scores = dot(recv[lo : lo + n, :], own, NT)
        tags = tag_col[lo : lo + n, :]
        allowed = jnp.concatenate([tags, tags], axis=1) == tag_row[0:1, t * CHUNK : (t + 1) * CHUNK]
        if diagonal:
            allowed = allowed & (iota((n, CHUNK), 0) != iota((n, CHUNK), 1))
        scores = jnp.where(allowed, scores, -1.0)
        row_max[lo : lo + n, :] = jnp.maximum(
            row_max[lo : lo + n, :], jnp.maximum(scores[:, :128], scores[:, 128:])
        )
        if diagonal:
            return jnp.full((8, CHUNK), -1.0, jnp.float32)
        return jnp.max(scores.reshape(n // 8, 8, CHUNK), axis=0)

    for t in range(CHUNKS):
        lo = 1 if t == 0 else t * GROUP
        n = (t + 1) * GROUP - lo
        whole(send, recv, (send_sem, recv_sem.at[t]), lo * SLOT, n * SLOT).wait_recv()
        whole(tag_out, tag_in, (tag_sems.at[0], tag_sems.at[1 + t]), lo, n).wait_recv()
        spread_tag = jnp.broadcast_to(tag_in[t * GROUP : (t + 1) * GROUP], (GROUP, SLOT, DEVS))
        tag = jnp.where(own_lane, spread_tag.reshape(CHUNK, DEVS), 0.0).astype(jnp.bfloat16)
        tag_col[t * CHUNK : (t + 1) * CHUNK, :] = dot(tag, jnp.ones((DEVS, DEVS), jnp.bfloat16))
        along = dot(jnp.ones((8, DEVS), jnp.bfloat16), tag, NT)
        tag_row[:, t * CHUNK : (t + 1) * CHUNK] = jnp.where(along == 0.0, -1.0, along)
        best = meet(t, t * CHUNK, CHUNK, True)
        for at in range(0, t * CHUNK, 512):
            best = jnp.maximum(best, meet(t, at, min(512, t * CHUNK - at), False))
        col_max[:, t * CHUNK : (t + 1) * CHUNK] = best

    eye = iota((128, 128), 0) == iota((128, 128), 1)
    for t in range(CHUNKS):
        along = jnp.max(col_max[:, t * CHUNK : (t + 1) * CHUNK], axis=0, keepdims=True)
        turned = jnp.concatenate(
            [jnp.where(eye, along[:, :128], -1.0), jnp.where(eye, along[:, 128:], -1.0)], axis=0
        )
        best = jnp.max(jnp.maximum(row_max[t * CHUNK : (t + 1) * CHUNK, :], turned), axis=1, keepdims=True)
        blocks = jnp.where(own_lane, best, -1.0).reshape(GROUP, SLOT, DEVS)
        laid[t * GROUP : (t + 1) * GROUP, :] = jnp.max(blocks, axis=1)

    def exact(rest, pick):
        total = None
        for _ in range(3):
            piece = rest.astype(jnp.bfloat16)
            rest = rest - piece.astype(jnp.float32)
            term = pick(piece)
            total = term if total is None else total + term
        return total

    best_out[...] = exact(laid[...], lambda piece: dot(to_source, piece)).reshape(DEVS, 1, DEVS)
    best_in[me] = best_out[me]
    for plane in range(4):
        for step in range(32):
            if step == 0:

                @pl.when(plane != z)
                def _():
                    best_copy(plane, 0, 0, 0).start()

            else:
                best_copy(plane, step >> 3, (step >> 1) & 3, step & 1).start()

    whole(send, recv, (send_sem, recv_sem.at[0]), SLOT, (DEVS - 1) * SLOT).wait_send()
    whole(tag_out, tag_in, (tag_sems.at[0], tag_sems.at[1]), 1, DEVS - 1).wait_send()
    whole(best_out, best_in, (best_sems.at[0], best_sems.at[1]), 1, DEVS - 1).wait()
    rank_bf = rank_is.astype(jnp.float32).astype(jnp.bfloat16)
    found = exact(best_in[...].reshape(DEVS, DEVS), lambda piece: dot(piece, rank_bf))
    owner = o_grp * 2 + o_mem
    out[...] = jnp.sum(jnp.where(iota((DEVS, rows), 0) == owner, found, 0.0), axis=0, keepdims=True)


def body(embeddings, cluster_of):
    rows, width = embeddings.shape
    slots = DEVS * SLOT
    best = pl.pallas_call(
        kernel,
        out_shape=jax.ShapeDtypeStruct((1, rows), jnp.float32),
        in_specs=[pl.BlockSpec(memory_space=pl.ANY)] * 2,
        out_specs=pl.BlockSpec(memory_space=pltpu.VMEM),
        scratch_shapes=[
            pltpu.VMEM((rows, width), jnp.float32),
            pltpu.VMEM((rows, width), jnp.bfloat16),
            pltpu.VMEM((slots, width), jnp.bfloat16),
            pltpu.VMEM((slots, width), jnp.bfloat16),
            pltpu.VMEM((DEVS, 1, DEVS), jnp.float32),
            pltpu.VMEM((DEVS, 1, DEVS), jnp.float32),
            pltpu.VMEM((DEVS, 1, DEVS), jnp.float32),
            pltpu.VMEM((DEVS, 1, DEVS), jnp.float32),
            pltpu.VMEM((slots, 128), jnp.float32),
            pltpu.VMEM((8, slots), jnp.float32),
            pltpu.VMEM((slots, 128), jnp.float32),
            pltpu.VMEM((8, slots), jnp.float32),
            pltpu.VMEM((1, rows), jnp.int32),
            pltpu.VMEM((DEVS, DEVS), jnp.float32),
            pltpu.SemaphoreType.DMA((9,)),
            pltpu.SemaphoreType.DMA,
            pltpu.SemaphoreType.DMA((CHUNKS,)),
            pltpu.SemaphoreType.DMA((1 + CHUNKS,)),
            pltpu.SemaphoreType.DMA((2,)),
            pltpu.SemaphoreType.REGULAR((2,)),
        ],
        compiler_params=pltpu.CompilerParams(
            collective_id=0, has_side_effects=True, vmem_limit_bytes=52 << 20
        ),
        cost_estimate=pl.CostEstimate(
            flops=2 * slots * slots * width, bytes_accessed=4 * rows * width, transcendentals=rows
        ),
        name="nearest",
    )(embeddings, cluster_of.reshape(1, rows))
    return best.reshape(rows)


def solution(mesh):
    return jax.shard_map(
        body,
        mesh=mesh,
        in_specs=(P(("grp", "mem"), None), P(("grp", "mem"))),
        out_specs=P(("grp", "mem")),
        check_vma=False,
    )
```

```python
import functools
import math

import jax
import jax.numpy as jnp
from jax import lax
from jax.experimental import pallas as pl
from jax.experimental.pallas import tpu as pltpu
from jax.sharding import PartitionSpec as P

MESH = pl.DeviceIdType.MESH
DEVS = 128


def axes(q):
    return (q >> 5 != 0) + ((q >> 3) & 3 != 0) + ((q >> 1) & 3 != 0)


LCG = [(107 * k) % DEVS for k in range(DEVS)]
def spread(a, b):
    n = len(a) + len(b)
    out, i = [], 0
    for k in range(n):
        if (k + 1) * len(a) // n > i:
            out.append(a[i])
            i += 1
        else:
            out.append(b[k - i])
    return out


ONE, TWO, THREE = ([q for q in LCG if q and max(1, axes(q)) == n] for n in (1, 2, 3))
ORDER = [0] + ONE + TWO[:24] + spread(TWO[24:], THREE)
SLOT = 16
GROUP = 16
CHUNK = GROUP * SLOT
CHUNKS = DEVS // GROUP
NT = (((1,), (1,)), ((), ()))


def dot(a, b, dims=(((1,), (0,)), ((), ()))):
    return lax.dot_general(a, b, dims, preferred_element_type=jnp.float32)


def iota(shape, dim):
    return lax.broadcasted_iota(jnp.int32, shape, dim)


def kernel(
    emb, ids_in, out,
    raw, normed, send, recv, tag_out, tag_in, best_out, best_in,
    tag_col, tag_row, row_max, col_max, ids, laid,
    load_sem, send_sem, recv_sem, tag_sems, best_sems, entry_sems,
):
    rows, width = raw.shape
    grp, core = lax.axis_index("grp"), lax.axis_index("mem")
    z, x, y = grp >> 4, (grp >> 2) & 3, grp & 3

    def lines(way):
        return [
            [((base + way * d) & 3) * scale for d in range(4)]
            for base, scale in ((z, 16), (x, 4), (y, 1))
        ]

    aways = lines(1 - 2 * core)
    aways = lines(1 - 2 * core)
    me = grp * 2 + core

    def away(k):
        q = ORDER[k]
        zs, xs, ys = aways
        return zs[q >> 5] + xs[(q >> 3) & 3] + ys[(q >> 1) & 3], core ^ (q & 1)

    part = rows // 8
    loads = [
        pltpu.make_async_copy(
            emb.at[pl.ds(i * part, part)], raw.at[pl.ds(i * part, part)], load_sem.at[i]
        )
        for i in range(8)
    ]
    ids_load = pltpu.make_async_copy(ids_in, ids, load_sem.at[8])
    ids_load.start()
    for load in loads:
        load.start()

    barrier = pltpu.get_barrier_semaphore()

    def greet(sem, other):
        pl.semaphore_signal(sem, inc=1, device_id=other, device_id_type=MESH)

    zs, xs, ys = aways
    z_line = [zs[d] + xs[0] + ys[0] for d in range(1, 4)]
    x_line = [zs[0] + xs[d] + ys[0] for d in range(1, 4)]
    y_line = [zs[0] + xs[0] + ys[d] for d in range(1, 4)]
    greet(barrier, (grp, core ^ 1))
    for chip in z_line + x_line + y_line:
        greet(barrier, (chip, core))
        greet(barrier, (chip, core ^ 1))

    def enter(stage):
        if stage == 1:
            pl.semaphore_wait(barrier, 19)
            for chip in z_line + x_line + y_line:
                greet(entry_sems.at[0], (chip, core))
        elif stage == 2:
            pl.semaphore_wait(entry_sems.at[0], 9)
            for chip in z_line:
                greet(entry_sems.at[1], (chip, core))
        else:
            pl.semaphore_wait(entry_sems.at[1], 3)

    lane = iota((1, DEVS), 1)
    parts = []
    for first in range(0, DEVS, 16):
        part_of = jnp.zeros((1, DEVS), jnp.int32)
        for k in range(first, first + 16):
            part_of = jnp.where(lane == k, ORDER[k], part_of)
        parts.append(part_of)
    shift = functools.reduce(jnp.add, parts)
    order = jnp.sum(
        jnp.where(iota((DEVS, DEVS), 0) == iota((DEVS, DEVS), 1), shift, 0).astype(jnp.float32),
        axis=1, keepdims=True,
    ).astype(jnp.int32)
    ids_load.wait()
    cluster = ids[...]
    o_grp, o_mem, layer = cluster & 63, (cluster >> 6) & 1, cluster >> 7
    way = 1 - 2 * core
    dz = (way * ((o_grp >> 4) - z)) & 3
    dx = (way * (((o_grp >> 2) & 3) - x)) & 3
    dy = (way * ((o_grp & 3) - y)) & 3
    dc = (o_mem - core) & 1
    there = core ^ (shift & 1)
    back = 2 * there - 1
    source = (
        ((z + back * (shift >> 5)) & 3) * 32
        + ((x + back * ((shift >> 3) & 3)) & 3) * 8
        + ((y + back * ((shift >> 1) & 3)) & 3) * 2
        + there
    )
    to_source = (iota((DEVS, DEVS), 0) == source).astype(jnp.float32).astype(jnp.bfloat16)
    owner_is = (order == dz * 32 + dx * 8 + dy * 2 + dc).astype(jnp.float32)
    owner_bf = owner_is.astype(jnp.bfloat16)
    upper = (iota((256, 256), 0) < iota((256, 256), 1)).astype(jnp.bfloat16)
    before = (iota((DEVS, 1), 0) * SLOT).astype(jnp.float32)
    slots = []
    for i in range(rows // 256):
        block = owner_is[:, i * 256 : (i + 1) * 256]
        ahead = dot(owner_bf[:, i * 256 : (i + 1) * 256], upper) + before
        slots.append(jnp.sum(block * ahead, axis=0, keepdims=True))
        before = before + jnp.sum(block, axis=1, keepdims=True)
    slot = jnp.concatenate(slots, axis=1).astype(jnp.int32)
    rank = slot & (SLOT - 1)
    rank_is = iota((DEVS, rows), 0) == rank
    tags = dot(
        owner_bf, jnp.where(rank_is, (layer + 1).astype(jnp.float32), 0.0).astype(jnp.bfloat16), NT
    )
    tag_out[...] = tags[:, :SLOT].reshape(DEVS, 1, SLOT)
    tag_in[0] = tag_out[0]

    for i in range(8):
        loads[i].wait()
        block = raw[i * part : (i + 1) * part, :]
        factor = lax.rsqrt(jnp.mean(block * block, axis=1, keepdims=True) + 1e-06) / math.sqrt(width)
        normed[i * part : (i + 1) * part, :] = (block * factor).astype(jnp.bfloat16)

    def row_copy(k, t):
        at = pl.ds(k * SLOT, SLOT)
        return pltpu.make_async_remote_copy(
            src_ref=send.at[at], dst_ref=recv.at[at], send_sem=send_sem, recv_sem=recv_sem.at[t],
            device_id=away(k), device_id_type=MESH,
        )

    def tag_copy(k):
        return pltpu.make_async_remote_copy(
            src_ref=tag_out.at[k], dst_ref=tag_in.at[k], send_sem=tag_sems.at[0], recv_sem=tag_sems.at[1 + k // GROUP],
            device_id=away(k), device_id_type=MESH,
        )

    def best_copy(plane, dx, dy, dc):
        chip, there = plane * 16 + xs[dx] + ys[dy], core ^ dc
        return pltpu.make_async_remote_copy(
            src_ref=best_out.at[chip * 2 + there], dst_ref=best_in.at[me],
            send_sem=best_sems.at[0], recv_sem=best_sems.at[1],
            device_id=(chip, there), device_id_type=MESH,
        )

    def whole(src, dst, sems, lo, n):
        return pltpu.make_async_remote_copy(
            src_ref=src.at[pl.ds(lo, n)], dst_ref=dst.at[pl.ds(lo, n)], send_sem=sems[0], recv_sem=sems[1],
            device_id=away(1), device_id_type=MESH,
        )

    stage = 0
    for t in range(CHUNKS):
        pick = (iota((CHUNK, rows), 0) + t * CHUNK == slot).astype(jnp.float32).astype(jnp.bfloat16)
        send[t * CHUNK : (t + 1) * CHUNK, :] = dot(pick, normed[...]).astype(jnp.bfloat16)
        if t == 0:
            recv[:SLOT, :] = send[:SLOT, :]
        for k in range(max(1, t * GROUP), (t + 1) * GROUP):
            need = max(1, axes(ORDER[k]))
            while stage < need:
                stage += 1
                enter(stage)
            tag_copy(k).start()
            row_copy(k, t).start()

    own_lane = iota((CHUNK, DEVS), 1) == iota((CHUNK, DEVS), 0) % SLOT
    row_max[...] = jnp.full(row_max.shape, -1.0, jnp.float32)

    def meet(t, lo, n, diagonal):
        own = recv[t * CHUNK : (t + 1) * CHUNK, :]
        scores = dot(recv[lo : lo + n, :], own, NT)
        tags = tag_col[lo : lo + n, :]
        allowed = jnp.concatenate([tags, tags], axis=1) == tag_row[0:1, t * CHUNK : (t + 1) * CHUNK]
        if diagonal:
            allowed = allowed & (iota((n, CHUNK), 0) != iota((n, CHUNK), 1))
        scores = jnp.where(allowed, scores, -1.0)
        row_max[lo : lo + n, :] = jnp.maximum(
            row_max[lo : lo + n, :], jnp.maximum(scores[:, :128], scores[:, 128:])
        )
        if diagonal:
            return jnp.full((8, CHUNK), -1.0, jnp.float32)
        return jnp.max(scores.reshape(n // 8, 8, CHUNK), axis=0)

    for t in range(CHUNKS):
        lo = 1 if t == 0 else t * GROUP
        n = (t + 1) * GROUP - lo
        whole(send, recv, (send_sem, recv_sem.at[t]), lo * SLOT, n * SLOT).wait_recv()
        whole(tag_out, tag_in, (tag_sems.at[0], tag_sems.at[1 + t]), lo, n).wait_recv()
        spread_tag = jnp.broadcast_to(tag_in[t * GROUP : (t + 1) * GROUP], (GROUP, SLOT, SLOT))
        tag = jnp.where(own_lane[:, :SLOT], spread_tag.reshape(CHUNK, SLOT), 0.0).astype(jnp.bfloat16)
        tag_col[t * CHUNK : (t + 1) * CHUNK, :] = dot(tag, jnp.ones((SLOT, DEVS), jnp.bfloat16))
        along = dot(jnp.ones((8, SLOT), jnp.bfloat16), tag, NT)
        tag_row[:, t * CHUNK : (t + 1) * CHUNK] = jnp.where(along == 0.0, -1.0, along)
        best = meet(t, t * CHUNK, CHUNK, True)
        for at in range(0, t * CHUNK, 512):
            best = jnp.maximum(best, meet(t, at, min(512, t * CHUNK - at), False))
        col_max[:, t * CHUNK : (t + 1) * CHUNK] = best

    eye = iota((128, 128), 0) == iota((128, 128), 1)
    for t in range(CHUNKS):
        along = jnp.max(col_max[:, t * CHUNK : (t + 1) * CHUNK], axis=0, keepdims=True)
        turned = jnp.concatenate(
            [jnp.where(eye, along[:, :128], -1.0), jnp.where(eye, along[:, 128:], -1.0)], axis=0
        )
        best = jnp.max(jnp.maximum(row_max[t * CHUNK : (t + 1) * CHUNK, :], turned), axis=1, keepdims=True)
        blocks = jnp.where(own_lane, best, -1.0).reshape(GROUP, SLOT, DEVS)
        laid[t * GROUP : (t + 1) * GROUP, :] = jnp.max(blocks, axis=1)

    def exact(rest, pick):
        total = None
        for _ in range(3):
            piece = rest.astype(jnp.bfloat16)
            rest = rest - piece.astype(jnp.float32)
            term = pick(piece)
            total = term if total is None else total + term
        return total

    best_out[...] = exact(laid[...], lambda piece: dot(to_source, piece))[:, :SLOT].reshape(DEVS, 1, SLOT)
    best_in[me] = best_out[me]
    for plane in range(4):
        for step in range(32):
            if step == 0:

                @pl.when(plane != z)
                def _():
                    best_copy(plane, 0, 0, 0).start()

            else:
                best_copy(plane, step >> 3, (step >> 1) & 3, step & 1).start()

    returns = whole(best_out, best_in, (best_sems.at[0], best_sems.at[1]), 1, DEVS - 1)
    returns.wait_recv()
    rank_bf = rank_is.astype(jnp.float32).astype(jnp.bfloat16)
    found = exact(best_in[...].reshape(DEVS, SLOT), lambda piece: dot(piece, rank_bf[:SLOT, :]))
    owner = o_grp * 2 + o_mem
    returns.wait_send()
    whole(send, recv, (send_sem, recv_sem.at[0]), SLOT, (DEVS - 1) * SLOT).wait_send()
    whole(tag_out, tag_in, (tag_sems.at[0], tag_sems.at[1]), 1, DEVS - 1).wait_send()
    out[...] = jnp.sum(jnp.where(iota((DEVS, rows), 0) == owner, found, 0.0), axis=0, keepdims=True)


def body(embeddings, cluster_of):
    rows, width = embeddings.shape
    slots = DEVS * SLOT
    best = pl.pallas_call(
        kernel,
        out_shape=jax.ShapeDtypeStruct((1, rows), jnp.float32),
        in_specs=[pl.BlockSpec(memory_space=pl.ANY)] * 2,
        out_specs=pl.BlockSpec(memory_space=pltpu.VMEM),
        scratch_shapes=[
            pltpu.VMEM((rows, width), jnp.float32),
            pltpu.VMEM((rows, width), jnp.bfloat16),
            pltpu.VMEM((slots, width), jnp.bfloat16),
            pltpu.VMEM((slots, width), jnp.bfloat16),
            pltpu.VMEM((DEVS, 1, SLOT), jnp.float32),
            pltpu.VMEM((DEVS, 1, SLOT), jnp.float32),
            pltpu.VMEM((DEVS, 1, SLOT), jnp.float32),
            pltpu.VMEM((DEVS, 1, SLOT), jnp.float32),
            pltpu.VMEM((slots, 128), jnp.float32),
            pltpu.VMEM((8, slots), jnp.float32),
            pltpu.VMEM((slots, 128), jnp.float32),
            pltpu.VMEM((8, slots), jnp.float32),
            pltpu.VMEM((1, rows), jnp.int32),
            pltpu.VMEM((DEVS, DEVS), jnp.float32),
            pltpu.SemaphoreType.DMA((9,)),
            pltpu.SemaphoreType.DMA,
            pltpu.SemaphoreType.DMA((CHUNKS,)),
            pltpu.SemaphoreType.DMA((1 + CHUNKS,)),
            pltpu.SemaphoreType.DMA((2,)),
            pltpu.SemaphoreType.REGULAR((2,)),
        ],
        compiler_params=pltpu.CompilerParams(
            collective_id=0, has_side_effects=True, vmem_limit_bytes=52 << 20
        ),
        cost_estimate=pl.CostEstimate(
            flops=2 * slots * slots * width, bytes_accessed=4 * rows * width, transcendentals=rows
        ),
        name="nearest",
    )(embeddings, cluster_of.reshape(1, rows))
    return best.reshape(rows)


def solution(mesh):
    return jax.shard_map(
        body,
        mesh=mesh,
        in_specs=(P(("grp", "mem"), None), P(("grp", "mem"))),
        out_specs=P(("grp", "mem")),
        check_vma=False,
    )
```
